32 devices in a mesh: seg: 4 (over y, core), pan: 8 (over z, x).
Axes of the slice: x: 2, y: 2, z: 4, core: 2. Of those that a mesh axis runs over, the one named last changes fastest.
Arguments:
- sources: bfloat16 [2, 2, 64, 65536], P(None, None, 'seg', 'pan'), may hold values from -3 to 3
- panel_geom: float32 [6, 65536], P(None, 'pan'), may hold values from -1 to 1, as said below
- mic_pos: float32 [3, 1024], replicated, may hold values from -12 to 12, as said below
- mic_order: int32 [1024], replicated, may hold values from 0 to 1023, each once
Outputs:
- csm: float32 [2, 1024, 1024], P(None, 'pan', 'seg')
The draws below stay inside these ranges and needn't reach their ends.
Inputs may be any that keep to these rules, and one draw needn't show every extreme that they name: `mic_order`: each of the 1024 microphones stands exactly once. `panel_geom`: panel centres lie on a cylinder of radius 1 around the first axis with first coordinate within -1 to 1; normals are the unit radial directions. `mic_pos`: microphones lie at distances 6 to 12 from the anchor (0, 0, 0).
All inputs are finite; a program needn't handle non-finite values.
Results may differ from the reference program's by a relative error of at most 0.0039.
Values may be sent and summed in bfloat16 or wider, within the bound.
A program may use at most 64 MiB of HBM per device.

```python
import math
import jax
import jax.numpy as jnp
from jax import lax

M = 1024
PAN_DEV = 8192
SEGS = 64
PANELS = 65536
N_PAN = 8


def draw_panel_geom(key, part):
    key_angle = jax.random.fold_in(key, 11)
    key_axial = jax.random.fold_in(key, 12)
    angle = jax.random.uniform(key_angle, (PANELS,), jnp.float32, -math.pi, math.pi)
    axial = jax.random.uniform(key_axial, (PANELS,), jnp.float32, -1.0, 1.0)
    cosine = jnp.cos(angle)
    sine = jnp.sin(angle)
    return jnp.stack([axial, cosine, sine, jnp.zeros_like(axial), cosine, sine]).astype(jnp.float32)


def draw_mic_pos(key, part):
    key_polar = jax.random.fold_in(key, 21)
    key_azimuth = jax.random.fold_in(key, 22)
    key_radius = jax.random.fold_in(key, 23)
    polar = jax.random.uniform(key_polar, (M,), jnp.float32, -1.0, 1.0)
    azimuth = jax.random.uniform(key_azimuth, (M,), jnp.float32, -math.pi, math.pi)
    radius = jax.random.uniform(key_radius, (M,), jnp.float32, 6.0, 12.0)
    across = jnp.sqrt(jnp.maximum(1.0 - polar * polar, 0.0))
    return jnp.stack([radius * polar, radius * across * jnp.cos(azimuth), radius * across * jnp.sin(azimuth)]).astype(jnp.float32)


def block_scale(key, extent, pieces, least, largest):
    loudness = 1.0
    for dim, blocks in pieces:
        draws = jax.random.uniform(jax.random.fold_in(jax.random.fold_in(key, 6), dim), (blocks,), jnp.float32, least / len(pieces), largest / len(pieces))
        loudness = loudness * jnp.repeat(jnp.exp(draws), extent[dim] // blocks).reshape((-1,) + (1,) * (len(extent) - 1 - dim))
    return loudness


def normal_values(rng, extent, scale, limit, cuts=(), held_as=jnp.bfloat16):
    level = block_scale(rng, extent, cuts, -0.22, 0.18) if cuts else 1.0
    values = jax.random.normal(rng, extent, jnp.float32) * scale * level
    return jnp.minimum(jnp.maximum(values, -limit), limit).astype(held_as)


def setup_inputs(seed: int = 0) -> dict:
    arg_keys = jax.random.split(jax.random.key(seed), 5)
    sources = normal_values(arg_keys[0], (2, 2, SEGS, PANELS), (50.0 / (PANELS ** 0.5)), 3.0, ((2, 4), (3, 8)))
    panel_geom = draw_panel_geom(jax.random.fold_in(arg_keys[4], 71), 0)
    mic_pos = draw_mic_pos(jax.random.fold_in(arg_keys[4], 71), 0)
    mic_order = jax.random.permutation(arg_keys[3], M).astype(jnp.int32)
    return {"sources": sources, "panel_geom": panel_geom, "mic_pos": mic_pos, "mic_order": mic_order}


mach_number = 0.3
beta_sq = 0.91
wave_number = 40.0

def kernel_block(mics, geometry):
    dx = mics[0][:, None] - geometry[0][None, :]
    dy = mics[1][:, None] - geometry[1][None, :]
    dz = mics[2][:, None] - geometry[2][None, :]
    rstar = jnp.sqrt(dx * dx + beta_sq * (dy * dy + dz * dz))
    radius = (rstar - mach_number * dx) / beta_sq
    phase = wave_number * radius
    amplitude = 1.0 / (4.0 * math.pi * rstar)
    green_re = amplitude * jnp.cos(phase)
    green_im = -amplitude * jnp.sin(phase)
    normal_part = (dx * geometry[3][None, :] + dy * geometry[4][None, :] + dz * geometry[5][None, :]) / rstar
    scale_re = normal_part / (wave_number * rstar)
    scale_im = normal_part
    dip_re = scale_re * green_re - scale_im * green_im
    dip_im = scale_re * green_im + scale_im * green_re
    return jnp.concatenate([green_re, green_im, dip_re, dip_im], axis=1).astype(jnp.bfloat16)

def build_sources(sources, blocks):
    swapped = jnp.transpose(sources, (0, 1, 3, 2))
    width = swapped.shape[2] // blocks
    swapped = swapped.reshape(2, 2, blocks, width, swapped.shape[3])
    mono_re = swapped[0, 0]
    dipole_re = swapped[0, 1]
    mono_im = swapped[1, 0]
    dipole_im = swapped[1, 1]
    real_cols = jnp.concatenate([mono_re, -mono_im, dipole_re, -dipole_im], axis=1)
    imag_cols = jnp.concatenate([mono_im, mono_re, dipole_im, dipole_re], axis=1)
    return jnp.concatenate([real_cols, imag_cols], axis=2)

def reference(sources, panel_geom, mic_pos, mic_order):
    ordered = jnp.take(mic_pos, mic_order, axis=1)
    geom_blocks = jnp.transpose(panel_geom.reshape(6, N_PAN, PAN_DEV), (1, 0, 2))
    source_blocks = build_sources(sources, N_PAN)

    def step(running, pair):
        geometry, weights = pair
        return (running + jnp.dot(kernel_block(ordered, geometry), weights, preferred_element_type=jnp.float32), None)
    init = jnp.zeros((ordered.shape[1], source_blocks.shape[2]), jnp.float32)
    spectra, unused = lax.scan(step, init, (geom_blocks, source_blocks))
    half = spectra.shape[1] // 2
    spec_re = spectra[:, :half]
    spec_im = spectra[:, half:]
    hp = lax.Precision.HIGHEST
    csm_re = jnp.dot(spec_re, spec_re.T, precision=hp) + jnp.dot(spec_im, spec_im.T, precision=hp)
    csm_im = jnp.dot(spec_im, spec_re.T, precision=hp) - jnp.dot(spec_re, spec_im.T, precision=hp)
    return jnp.stack([csm_re, csm_im]) / SEGS
```

```python
import functools
import math

import jax
import jax.numpy as jnp
import numpy as np
from jax import lax
from jax.experimental import pallas as pl
from jax.experimental.pallas import tpu as pltpu
from jax.sharding import PartitionSpec as P

mach_number = 0.3
beta_sq = 0.91
wave_number = 40.0

MESH = pl.DeviceIdType.MESH
LANES = 128
SUB_ROWS = 32
TURN = wave_number / (beta_sq * 2.0 * math.pi)
BETA = math.sqrt(beta_sq)


def fit(function, degree_even, half_range, odd):
    count = degree_even + 1
    nodes = np.cos((np.arange(200) + 0.5) * math.pi / 200)
    u = (nodes + 1) / 2 * half_range**2
    x = np.sqrt(u)
    y = function(x) / x if odd else function(x)
    cheb = np.polynomial.chebyshev.Chebyshev.fit(
        u, y, count - 1, domain=[0, half_range**2]
    )
    return [float(v) for v in cheb.convert(kind=np.polynomial.Polynomial).coef]


ROOT2 = math.sqrt(2.0)
SIN_COEF = fit(lambda x: ROOT2 * np.sin(math.pi * x), 4, 0.5, True)
COS_COEF = fit(lambda x: ROOT2 * np.cos(math.pi * x), 4, 0.5, False)


def horner(coef, u):
    total = coef[-1]
    for c in coef[-2::-1]:
        total = total * u + c
    return total


def pair_terms(mx, my, mz, panel):
    cx, cy, cz, n0, n1, n2 = panel
    dx = mx - cx
    dy = my - cy
    dz = mz - cz
    sq = dx * dx + (dy * dy + dz * dz)
    inv = lax.rsqrt(sq)
    turns = sq * inv - mach_number * dx
    magic = 12582912.0
    whole = (turns + magic) - magic
    f = turns - whole
    u = f * f
    s = horner(SIN_COEF, u) * f
    c = horner(COS_COEF, u)
    amplitude = inv * (TURN / (4.0 * math.pi))
    green_re = amplitude * (1.0 - s * s)
    green_im_neg = amplitude * (s * c)
    normal_part = (dx * n0 + (dy * n1 + dz * n2)) * inv
    near = inv * (TURN / wave_number)
    dip_re = normal_part * (near * green_re + green_im_neg)
    dip_im = normal_part * (green_re - near * green_im_neg)
    return green_re, -green_im_neg, dip_re, dip_im


def kernel(cfg, src, geom, mics, order, out, src_buf, geo, micb, g_buf, r1, r2, spec,
           rs_buf, own, cols, rows, loc_sem, core_sems, y_send, y_recv, f_send, f_recv,
           rs_send, rs_recv, col_send, col_recv, row_send, row_recv):
    n_seg, n_pan, segs_here, half, block, chunk, n_own, rows_per, pieces = cfg
    n_split = n_seg // 2
    n_red = n_split * n_pan
    n_row_chunks = rows_per // chunk
    s = lax.axis_index("seg")
    p = lax.axis_index("pan")
    y = s // 2
    c = lax.rem(s, 2)
    me = y * n_pan + p
    core_peer = (y * 2 + 1 - c, p)
    m_own = s * block + chunk * p
    p_r = m_own // rows_per
    row_slot = (m_own - p_r * rows_per) // chunk
    owner = p < n_own

    def row_owner(k):
        m = rows_per * p + chunk * k
        so = m // block
        return so, (m - so * block) // chunk

    barrier = pltpu.get_barrier_semaphore()

    def tell(k, carry):
        t = lax.rem(me + k, n_red)
        pl.semaphore_signal(barrier, inc=1, device_id=((t // n_pan) * 2 + c, lax.rem(t, n_pan)),
                            device_id_type=MESH)
        return carry

    lax.fori_loop(1, n_red, tell, 0)
    pl.semaphore_signal(barrier, inc=1, device_id=core_peer, device_id_type=MESH)
    for k in range(n_row_chunks):
        so, po = row_owner(k)

        @pl.when(jnp.logical_or(so != s, po != p))
        def _():
            pl.semaphore_signal(barrier, inc=1, device_id=(so, po), device_id_type=MESH)

    positions = mics[...]
    part1 = positions.astype(jnp.bfloat16)
    rest = positions - part1.astype(jnp.float32)
    part2 = rest.astype(jnp.bfloat16)
    part3 = (rest - part2.astype(jnp.float32)).astype(jnp.bfloat16)
    n_mic = positions.shape[1]
    for b in range(n_split):
        listed = order[:, pl.ds(pl.multiple_of((2 * b + c) * block, LANES), block)]
        hot = (lax.broadcasted_iota(jnp.int32, (n_mic, block), 0) == listed)
        hot = jnp.where(hot, 1.0, 0.0).astype(jnp.bfloat16)
        chosen = sum(jnp.dot(q, hot, preferred_element_type=jnp.float32)
                     for q in (part1, part2, part3))
        for axis in range(3):
            scaled = chosen[axis:axis + 1] * (TURN if axis == 0 else TURN * BETA)
            for at in range(0, block, LANES):
                tile = jnp.broadcast_to(scaled[:, at:at + LANES], (LANES, LANES))
                micb[axis, pl.ds(b * block + at, LANES), :] = tile.T
    here = pl.ds(pl.multiple_of(y * half, LANES), half)
    for r, scale in enumerate((TURN, TURN * BETA, TURN * BETA, 1.0, 1.0 / BETA, 1.0 / BETA)):
        geo[r:r + 1, :] = geom[r:r + 1, here] * scale

    own_rows_sent = jnp.where(p_r == p, n_seg - 1, n_seg)
    if n_own < n_pan:
        own_rows_sent = jnp.where(owner, own_rows_sent, 0)
    pl.semaphore_wait(barrier, n_red + own_rows_sent)

    def seg_rows(index):
        return pl.ds(pl.multiple_of(index * segs_here, 16), segs_here)

    piece = half // pieces

    def y_copy(k, j):
        yy = lax.rem(y + k, n_split)
        start = pl.multiple_of(yy * half + j * piece, LANES)
        return pltpu.make_async_remote_copy(
            src_ref=src.at[:, :, :, pl.ds(start, piece)],
            dst_ref=src_buf.at[:, :, seg_rows(s), pl.ds(j * piece, piece)],
            send_sem=y_send.at[k - 1, j], recv_sem=y_recv.at[k - 1, j],
            device_id=(yy * 2 + c, p), device_id_type=MESH)

    def y_from(k):
        return lax.rem(y + n_split - k, n_split) * 2 + c

    def forward(k, j, cc):
        at = lax.rem(y + n_split - k, n_split) * 2 + cc
        ref = src_buf.at[:, :, seg_rows(at), pl.ds(j * piece, piece)]
        return pltpu.make_async_remote_copy(
            src_ref=ref, dst_ref=ref, send_sem=f_send.at[k - 1, j], recv_sem=f_recv.at[k - 1, j],
            device_id=core_peer, device_id_type=MESH)

    for j in range(pieces):
        for k in range(1, n_split):
            y_copy(k, j).start()
    core_copy = pltpu.make_async_remote_copy(
        src_ref=src.at[:, :, :, here], dst_ref=src_buf.at[:, :, seg_rows(s), :],
        send_sem=core_sems.at[0], recv_sem=core_sems.at[1],
        device_id=core_peer, device_id_type=MESH)
    core_copy.start()
    local_copy = pltpu.make_async_copy(
        src.at[:, :, :, here], src_buf.at[:, :, seg_rows(s), :], loc_sem.at[0])
    local_copy.start()

    mic_here = n_split * block
    body_rows = min(256, mic_here)
    parts = mic_here // body_rows

    def pairs(step, carry):
        lane = pl.multiple_of((step // parts) * LANES, LANES)
        base = lax.rem(step, parts) * body_rows
        panel = [jnp.broadcast_to(geo[r:r + 1, pl.ds(lane, LANES)], (SUB_ROWS, LANES))
                 for r in range(6)]
        for q in range(body_rows // SUB_ROWS):
            at = pl.ds(pl.multiple_of(base + q * SUB_ROWS, SUB_ROWS), SUB_ROWS)
            terms = pair_terms(micb[0, at, :], micb[1, at, :], micb[2, at, :], panel)
            for i in range(4):
                g_buf[i, at, pl.ds(lane, LANES)] = terms[i].astype(jnp.bfloat16)
        return carry

    steps = (piece // LANES) * parts
    for j in range(pieces):
        lax.fori_loop(j * steps, (j + 1) * steps, pairs, 0)
        for k in range(1, n_split):
            y_copy(k, j).wait_recv()
            forward(k, j, c).start()

    local_copy.wait()
    core_copy.wait()
    nt = (((1,), (1,)), ((), ()))
    for j in range(pieces):
        for k in range(1, n_split):
            y_copy(k, j).wait_send()
            forward(k, j, c).wait_send()
            forward(k, j, 1 - c).wait_recv()
        at = pl.ds(j * piece, piece)
        mono = jnp.concatenate([src_buf[0, 0, :, at], src_buf[1, 0, :, at]], axis=0)
        dipole = jnp.concatenate([src_buf[0, 1, :, at], src_buf[1, 1, :, at]], axis=0)
        for first, total in ((0, r1), (1, r2)):
            term = lax.dot_general(g_buf[first, :, at], mono, nt,
                                   preferred_element_type=jnp.float32)
            term += lax.dot_general(g_buf[first + 2, :, at], dipole, nt,
                                    preferred_element_type=jnp.float32)
            total[...] = term if j == 0 else total[...] + term

    n_all = n_seg * segs_here
    for b in range(n_split):
        band = pl.ds(b * block, block)
        spec[b, :, :n_all] = r1[band, :n_all] - r2[band, n_all:]
        spec[b, :, n_all:] = r1[band, n_all:] + r2[band, :n_all]

    def rs_copy(t):
        ty = t // n_pan
        tp = lax.rem(t, n_pan)
        return tp, pltpu.make_async_remote_copy(
            src_ref=spec.at[ty, pl.ds(pl.multiple_of(tp * chunk, 8), chunk)],
            dst_ref=rs_buf.at[me], send_sem=rs_send.at[t], recv_sem=rs_recv.at[me],
            device_id=(ty * 2 + c, tp), device_id_type=MESH)

    def each_rs(action):
        def go(k, carry):
            tp, copy = rs_copy(lax.rem(me + k, n_red))
            if n_own < n_pan:
                pl.when(tp < n_own)(lambda: action(copy))
            else:
                action(copy)
            return carry

        lax.fori_loop(1, n_red, go, 0)

    each_rs(lambda copy: copy.start())

    def own_slot(ref):
        return ref.at[pl.ds(pl.multiple_of(p * chunk, 8), chunk)]

    def col_copy(q):
        return pltpu.make_async_remote_copy(
            src_ref=own, dst_ref=own_slot(cols), send_sem=col_send.at[q], recv_sem=col_recv.at[p],
            device_id=(s, q), device_id_type=MESH)

    def row_copy(q):
        return pltpu.make_async_remote_copy(
            src_ref=own, dst_ref=rows.at[pl.ds(pl.multiple_of(row_slot * chunk, 8), chunk)],
            send_sem=row_send.at[q], recv_sem=row_recv.at[row_slot],
            device_id=(q, p_r), device_id_type=MESH)

    def each_col(action):
        def go(k, carry):
            action(lax.rem(p + k, n_pan))
            return carry

        lax.fori_loop(1, n_pan, go, 0)

    def each_row(action):
        for k in range(n_seg):
            q = lax.rem(s + k, n_seg)
            if k == 0:
                pl.when(p_r != p)(lambda: action(row_copy(q)))
            else:
                action(row_copy(q))

    def own_sum():
        rs_buf[me] = spec[y, pl.ds(pl.multiple_of(p * chunk, 8), chunk), :]

        def arrived(k, carry):
            t = lax.rem(me + k, n_red)
            pltpu.make_async_remote_copy(
                src_ref=rs_buf.at[t], dst_ref=rs_buf.at[t], send_sem=rs_send.at[t],
                recv_sem=rs_recv.at[t], device_id=core_peer, device_id_type=MESH).wait_recv()
            return carry

        lax.fori_loop(1, n_red, arrived, 0)
        own[...] = jnp.sum(rs_buf[...], axis=0)
        each_col(lambda q: col_copy(q).start())
        each_row(lambda copy: copy.start())
        cols[pl.ds(pl.multiple_of(p * chunk, 8), chunk), :] = own[...]

        @pl.when(p_r == p)
        def _():
            rows[pl.ds(pl.multiple_of(row_slot * chunk, 8), chunk), :] = own[...]

    def own_done():
        each_col(lambda q: col_copy(q).wait_send())
        each_row(lambda copy: copy.wait_send())

    if n_own < n_pan:
        pl.when(owner)(own_sum)
    else:
        own_sum()

    each_rs(lambda copy: copy.wait_send())

    def col_arrived(k, carry):
        q = lax.rem(p + k, n_pan)

        def wait():
            slot = cols.at[pl.ds(pl.multiple_of(q * chunk, 8), chunk)]
            pltpu.make_async_remote_copy(
                src_ref=slot, dst_ref=slot, send_sem=col_send.at[q], recv_sem=col_recv.at[q],
                device_id=core_peer, device_id_type=MESH).wait_recv()

        if n_own < n_pan:
            pl.when(q < n_own)(wait)
        else:
            wait()
        return carry

    lax.fori_loop(1, n_pan, col_arrived, 0)
    for k in range(n_row_chunks):
        so, po = row_owner(k)

        @pl.when(jnp.logical_or(so != s, po != p))
        def _():
            slot = rows.at[pl.ds(k * chunk, chunk)]
            pltpu.make_async_remote_copy(
                src_ref=slot, dst_ref=slot, send_sem=row_send.at[0], recv_sem=row_recv.at[k],
                device_id=core_peer, device_id_type=MESH).wait_recv()

    row_spec = rows[...]
    col_spec = cols[...]
    turned = jnp.concatenate([row_spec[:, n_all:], -row_spec[:, :n_all]], axis=1)
    highest = lax.Precision.HIGHEST
    out[0] = lax.dot_general(row_spec, col_spec, nt, precision=highest,
                             preferred_element_type=jnp.float32) * (1.0 / n_all)
    out[1] = lax.dot_general(turned, col_spec, nt, precision=highest,
                             preferred_element_type=jnp.float32) * (1.0 / n_all)
    if n_own < n_pan:
        pl.when(owner)(own_done)
    else:
        own_done()


def shards(sources, panel_geom, mic_pos, mic_order):
    n_seg = lax.axis_size("seg")
    n_pan = lax.axis_size("pan")
    segs_here = sources.shape[2]
    panels = sources.shape[3]
    n_mic = mic_pos.shape[1]
    n_split = n_seg // 2
    half = panels // n_split
    block = n_mic // n_seg
    chunk = max(8, block // n_pan)
    n_own = block // chunk
    rows_per = n_mic // n_pan
    n_red = n_split * n_pan
    width = 2 * n_seg * segs_here
    pieces = 4
    cfg = (n_seg, n_pan, segs_here, half, block, chunk, n_own, rows_per, pieces)
    f32, bf16 = jnp.float32, jnp.bfloat16
    dma = pltpu.SemaphoreType.DMA
    vmem = pl.BlockSpec(memory_space=pltpu.VMEM)
    mic_here = n_split * block
    return pl.pallas_call(
        functools.partial(kernel, cfg),
        out_shape=jax.ShapeDtypeStruct((2, rows_per, block), f32),
        in_specs=[pl.BlockSpec(memory_space=pl.ANY), vmem, vmem, vmem],
        out_specs=vmem,
        scratch_shapes=[
            pltpu.VMEM((2, 2, n_seg * segs_here, half), bf16),
            pltpu.VMEM((8, half), f32),
            pltpu.VMEM((3, mic_here, LANES), f32),
            pltpu.VMEM((4, mic_here, half), bf16),
            pltpu.VMEM((mic_here, width), f32),
            pltpu.VMEM((mic_here, width), f32),
            pltpu.VMEM((n_split, block, width), f32),
            pltpu.VMEM((n_red, chunk, width), f32),
            pltpu.VMEM((chunk, width), f32),
            pltpu.VMEM((block, width), f32),
            pltpu.VMEM((rows_per, width), f32),
            dma((1,)), dma((2,)),
            dma((n_split - 1, pieces)), dma((n_split - 1, pieces)),
            dma((n_split - 1, pieces)), dma((n_split - 1, pieces)),
            dma((n_red,)), dma((n_red,)),
            dma((n_pan,)), dma((n_pan,)),
            dma((n_seg,)), dma((rows_per // chunk,)),
        ],
        compiler_params=pltpu.CompilerParams(
            collective_id=0, has_side_effects=True, vmem_limit_bytes=48 * 2**20),
        cost_estimate=pl.CostEstimate(
            flops=2 * 4 * mic_here * half * width, bytes_accessed=2**21,
            transcendentals=mic_here * half),
    )(sources, panel_geom, mic_pos, mic_order.reshape(1, n_mic))


def solution(mesh):
    placed = (P(None, None, "seg", "pan"), P(None, "pan"), P(), P())
    return jax.shard_map(
        shards, mesh=mesh, in_specs=placed, out_specs=P(None, "pan", "seg"), check_vma=False
    )
```

```python
import functools
import math

import jax
import jax.numpy as jnp
import numpy as np
from jax import lax
from jax.experimental import pallas as pl
from jax.experimental.pallas import tpu as pltpu
from jax.sharding import PartitionSpec as P

mach_number = 0.3
beta_sq = 0.91
wave_number = 40.0

MESH = pl.DeviceIdType.MESH
LANES = 128
SUB_ROWS = 32
LAG = 3
TURN = wave_number / (beta_sq * 2.0 * math.pi)
BETA = math.sqrt(beta_sq)


def fit(function, degree_even, half_range, odd):
    count = degree_even + 1
    nodes = np.cos((np.arange(200) + 0.5) * math.pi / 200)
    u = (nodes + 1) / 2 * half_range**2
    x = np.sqrt(u)
    y = function(x) / x if odd else function(x)
    cheb = np.polynomial.chebyshev.Chebyshev.fit(
        u, y, count - 1, domain=[0, half_range**2]
    )
    return [float(v) for v in cheb.convert(kind=np.polynomial.Polynomial).coef]


ROOT2 = math.sqrt(2.0)
SIN_COEF = fit(lambda x: -ROOT2 * np.sin(math.pi * x), 3, 0.5, True)
COS_COEF = fit(lambda x: ROOT2 * np.cos(math.pi * x), 4, 0.5, False)


def horner(coef, u):
    total = coef[-1]
    for c in coef[-2::-1]:
        total = total * u + c
    return total


def pair_terms(mx, my, mz, panel):
    cx, cy, cz, n0, n1, n2 = panel
    dx = mx - cx
    dy = my - cy
    dz = mz - cz
    sq = dx * dx + (dy * dy + dz * dz)
    inv = lax.rsqrt(sq)
    turns = sq * inv - mach_number * dx
    magic = 12582912.0
    whole = (turns + magic) - magic
    f = turns - whole
    u = f * f
    s = horner(SIN_COEF, u) * f
    c = horner(COS_COEF, u)
    amplitude = inv * (TURN / (4.0 * math.pi))
    green_re = amplitude * (1.0 - s * s)
    green_im = amplitude * (s * c)
    normal_part = (dx * n0 + (dy * n1 + dz * n2)) * inv
    near = inv * (TURN / wave_number)
    dip_re = normal_part * (near * green_re - green_im)
    dip_im = normal_part * (near * green_im + green_re)
    return green_re, green_im, dip_re, dip_im


def kernel(cfg, src, geom_hbm, mics_hbm, order_hbm, out, src_buf, geom, mics, order, geo, micb,
           g_even, g_odd, r1, r2, spec, rs_buf, own, cols, rows, loc_sem, core_sems, y_send, y_recv, f_send, f_recv,
           rs_send, rs_recv, col_send, col_recv, row_send, row_recv):
    n_seg, n_pan, segs_here, half, block, chunk, n_own, rows_per, pieces = cfg
    n_split = n_seg // 2
    n_red = n_split * n_pan
    n_row_chunks = rows_per // chunk
    s = lax.axis_index("seg")
    p = lax.axis_index("pan")
    y = s // 2
    c = lax.rem(s, 2)
    me = y * n_pan + p
    core_peer = (y * 2 + 1 - c, p)
    m_own = s * block + chunk * p
    p_r = m_own // rows_per
    row_slot = (m_own - p_r * rows_per) // chunk
    owner = p < n_own

    def row_owner(k):
        m = rows_per * p + chunk * k
        so = m // block
        return so, (m - so * block) // chunk

    barrier = pltpu.get_barrier_semaphore()

    def tell(k, carry):
        t = lax.rem(me + k, n_red)
        pl.semaphore_signal(barrier, inc=1, device_id=((t // n_pan) * 2 + c, lax.rem(t, n_pan)),
                            device_id_type=MESH)
        return carry

    lax.fori_loop(1, n_red, tell, 0)
    pl.semaphore_signal(barrier, inc=1, device_id=core_peer, device_id_type=MESH)
    for k in range(n_row_chunks):
        so, po = row_owner(k)

        @pl.when(jnp.logical_or(so != s, po != p))
        def _():
            pl.semaphore_signal(barrier, inc=1, device_id=(so, po), device_id_type=MESH)

    here = pl.ds(pl.multiple_of(y * half, LANES), half)
    fetches = [
        pltpu.make_async_copy(order_hbm, order, loc_sem.at[1]),
        pltpu.make_async_copy(mics_hbm, mics, loc_sem.at[2]),
        pltpu.make_async_copy(geom_hbm.at[:, here], geom, loc_sem.at[3]),
    ]
    for fetch in fetches:
        fetch.start()
    for fetch in fetches:
        fetch.wait()

    positions = mics[...]
    part1 = positions.astype(jnp.bfloat16)
    rest = positions - part1.astype(jnp.float32)
    part2 = rest.astype(jnp.bfloat16)
    part3 = (rest - part2.astype(jnp.float32)).astype(jnp.bfloat16)
    n_mic = positions.shape[1]
    for b in range(n_split):
        listed = order[:, pl.ds(pl.multiple_of((2 * b + c) * block, LANES), block)]
        hot = (lax.broadcasted_iota(jnp.int32, (n_mic, block), 0) == listed)
        hot = jnp.where(hot, 1.0, 0.0).astype(jnp.bfloat16)
        chosen = sum(jnp.dot(q, hot, preferred_element_type=jnp.float32)
                     for q in (part1, part2, part3))
        for axis in range(3):
            scaled = chosen[axis:axis + 1] * (TURN if axis == 0 else TURN * BETA)
            for at in range(0, block, LANES):
                tile = jnp.broadcast_to(scaled[:, at:at + LANES], (LANES, LANES))
                micb[axis, pl.ds(b * block + at, LANES), :] = tile.T
    r1[...] = jnp.zeros_like(r1)
    r2[...] = jnp.zeros_like(r2)
    for r, scale in enumerate((TURN, TURN * BETA, TURN * BETA, 1.0, 1.0 / BETA, 1.0 / BETA)):
        geo[r:r + 1, :] = geom[r:r + 1, :] * scale

    own_rows_sent = jnp.where(p_r == p, n_seg - 1, n_seg)
    if n_own < n_pan:
        own_rows_sent = jnp.where(owner, own_rows_sent, 0)
    pl.semaphore_wait(barrier, n_red + own_rows_sent)

    def seg_rows(index):
        return pl.ds(pl.multiple_of(index * segs_here, 16), segs_here)

    piece = half // pieces

    def y_copy(k, j):
        yy = lax.rem(y + k, n_split)
        start = pl.multiple_of(yy * half + j * piece, LANES)
        return pltpu.make_async_remote_copy(
            src_ref=src.at[:, :, :, pl.ds(start, piece)],
            dst_ref=src_buf.at[:, :, seg_rows(s), pl.ds(pl.multiple_of(j * piece, LANES), piece)],
            send_sem=y_send.at[k - 1, j], recv_sem=y_recv.at[k - 1, j],
            device_id=(yy * 2 + c, p), device_id_type=MESH)

    def y_from(k):
        return lax.rem(y + n_split - k, n_split) * 2 + c

    def forward(k, j, cc):
        at = lax.rem(y + n_split - k, n_split) * 2 + cc
        ref = src_buf.at[:, :, seg_rows(at), pl.ds(pl.multiple_of(j * piece, LANES), piece)]
        return pltpu.make_async_remote_copy(
            src_ref=ref, dst_ref=ref, send_sem=f_send.at[k - 1, j], recv_sem=f_recv.at[k - 1, j],
            device_id=core_peer, device_id_type=MESH)

    def start_y(j, carry):
        for k in range(1, n_split):
            y_copy(k, j).start()
        return carry

    lax.fori_loop(0, pieces, start_y, 0)
    core_copy = pltpu.make_async_remote_copy(
        src_ref=src.at[:, :, :, here], dst_ref=src_buf.at[:, :, seg_rows(s), :],
        send_sem=core_sems.at[0], recv_sem=core_sems.at[1],
        device_id=core_peer, device_id_type=MESH)
    core_copy.start()
    local_copy = pltpu.make_async_copy(
        src.at[:, :, :, here], src_buf.at[:, :, seg_rows(s), :], loc_sem.at[0])
    local_copy.start()

    mic_here = n_split * block
    body_rows = min(256, mic_here)
    nt = (((1,), (1,)), ((), ()))

    def slot_lanes(j):
        return (j // 2) * piece

    def products(j, g_ref, band):
        at = pl.ds(pl.multiple_of(j * piece, LANES), piece)
        slot = pl.ds(pl.multiple_of(slot_lanes(j), LANES), piece)
        mono = jnp.concatenate([src_buf[0, 0, :, at], src_buf[1, 0, :, at]], axis=0)
        dipole = jnp.concatenate([src_buf[0, 1, :, at], src_buf[1, 1, :, at]], axis=0)
        for first, total in ((0, r1), (1, r2)):
            term = lax.dot_general(g_ref[first, band, slot], mono, nt,
                                   preferred_element_type=jnp.float32)
            term += lax.dot_general(g_ref[first + 2, band, slot], dipole, nt,
                                    preferred_element_type=jnp.float32)
            total[band, :] += term

    def pairs(j, g_ref, base):
        for lane in range(0, piece, LANES):
            read = pl.ds(pl.multiple_of(j * piece + lane, LANES), LANES)
            write = pl.ds(pl.multiple_of(slot_lanes(j) + lane, LANES), LANES)
            panel = [jnp.broadcast_to(geo[r:r + 1, read], (SUB_ROWS, LANES)) for r in range(6)]
            for q in range(body_rows // SUB_ROWS):
                at = pl.ds(pl.multiple_of(base + q * SUB_ROWS, SUB_ROWS), SUB_ROWS)
                terms = pair_terms(micb[0, at, :], micb[1, at, :], micb[2, at, :], panel)
                for i in range(4):
                    g_ref[i, at, write] = terms[i].astype(jnp.bfloat16)

    g_refs = (g_even, g_odd)

    def unit(j, parity, with_pairs, with_products):
        if with_products:
            for k in range(1, n_split):
                forward(k, j - LAG, 1 - c).wait_recv()

        def band_step(h, carry):
            base = pl.multiple_of(h * body_rows, body_rows)
            if with_products:
                products(j - LAG, g_refs[1 - parity], pl.ds(base, body_rows))
            if with_pairs:
                pairs(j, g_refs[parity], base)
            return carry

        lax.fori_loop(0, mic_here // body_rows, band_step, 0)

    def pass_on(j):
        for k in range(1, n_split):
            y_copy(k, j).wait_recv()
            forward(k, j, c).start()

    for j in range(LAG):
        unit(j, j % 2, True, False)
        if j > 0:
            pass_on(j - 1)
    local_copy.wait()
    core_copy.wait()

    def two_units(i, carry):
        for extra in range(2):
            j = LAG + 2 * i + extra
            unit(j, (LAG + extra) % 2, True, True)
            pass_on(j - 1)
        return carry

    lax.fori_loop(0, (pieces - LAG - 1) // 2, two_units, 0)
    unit(pieces - 1, (pieces - 1) % 2, True, True)
    pass_on(pieces - 2)
    pass_on(pieces - 1)
    for j in range(pieces, pieces + LAG):
        unit(j, j % 2, False, True)

    def sent(j, carry):
        for k in range(1, n_split):
            y_copy(k, j).wait_send()
            forward(k, j, c).wait_send()
        return carry

    lax.fori_loop(0, pieces, sent, 0)

    n_all = n_seg * segs_here
    for b in range(n_split):
        band = pl.ds(b * block, block)
        spec[b, :, :n_all] = r1[band, :n_all] - r2[band, n_all:]
        spec[b, :, n_all:] = r1[band, n_all:] + r2[band, :n_all]

    def rs_copy(t):
        ty = t // n_pan
        tp = lax.rem(t, n_pan)
        return tp, pltpu.make_async_remote_copy(
            src_ref=spec.at[ty, pl.ds(pl.multiple_of(tp * chunk, 8), chunk)],
            dst_ref=rs_buf.at[me], send_sem=rs_send.at[t], recv_sem=rs_recv.at[me],
            device_id=(ty * 2 + c, tp), device_id_type=MESH)

    def each_rs(action):
        def go(k, carry):
            tp, copy = rs_copy(lax.rem(me + k, n_red))
            if n_own < n_pan:
                pl.when(tp < n_own)(lambda: action(copy))
            else:
                action(copy)
            return carry

        lax.fori_loop(1, n_red, go, 0)

    each_rs(lambda copy: copy.start())

    def own_slot(ref):
        return ref.at[pl.ds(pl.multiple_of(p * chunk, 8), chunk)]

    def col_copy(q):
        return pltpu.make_async_remote_copy(
            src_ref=own, dst_ref=own_slot(cols), send_sem=col_send.at[q], recv_sem=col_recv.at[p],
            device_id=(s, q), device_id_type=MESH)

    def row_copy(q):
        return pltpu.make_async_remote_copy(
            src_ref=own, dst_ref=rows.at[pl.ds(pl.multiple_of(row_slot * chunk, 8), chunk)],
            send_sem=row_send.at[q], recv_sem=row_recv.at[row_slot],
            device_id=(q, p_r), device_id_type=MESH)

    def each_col(action):
        def go(k, carry):
            action(lax.rem(p + k, n_pan))
            return carry

        lax.fori_loop(1, n_pan, go, 0)

    def each_row(action):
        for k in range(n_seg):
            q = lax.rem(s + k, n_seg)
            if k == 0:
                pl.when(p_r != p)(lambda: action(row_copy(q)))
            else:
                action(row_copy(q))

    def own_sum():
        rs_buf[me] = spec[y, pl.ds(pl.multiple_of(p * chunk, 8), chunk), :]

        def arrived(k, carry):
            t = lax.rem(me + k, n_red)
            pltpu.make_async_remote_copy(
                src_ref=rs_buf.at[t], dst_ref=rs_buf.at[t], send_sem=rs_send.at[t],
                recv_sem=rs_recv.at[t], device_id=core_peer, device_id_type=MESH).wait_recv()
            return carry

        lax.fori_loop(1, n_red, arrived, 0)
        own[...] = jnp.sum(rs_buf[...], axis=0)
        each_col(lambda q: col_copy(q).start())
        each_row(lambda copy: copy.start())
        cols[pl.ds(pl.multiple_of(p * chunk, 8), chunk), :] = own[...]

        @pl.when(p_r == p)
        def _():
            rows[pl.ds(pl.multiple_of(row_slot * chunk, 8), chunk), :] = own[...]

    def own_done():
        each_col(lambda q: col_copy(q).wait_send())
        each_row(lambda copy: copy.wait_send())

    if n_own < n_pan:
        pl.when(owner)(own_sum)
    else:
        own_sum()

    each_rs(lambda copy: copy.wait_send())

    def col_arrived(k, carry):
        q = lax.rem(p + k, n_pan)

        def wait():
            slot = cols.at[pl.ds(pl.multiple_of(q * chunk, 8), chunk)]
            pltpu.make_async_remote_copy(
                src_ref=slot, dst_ref=slot, send_sem=col_send.at[q], recv_sem=col_recv.at[q],
                device_id=core_peer, device_id_type=MESH).wait_recv()

        if n_own < n_pan:
            pl.when(q < n_own)(wait)
        else:
            wait()
        return carry

    lax.fori_loop(1, n_pan, col_arrived, 0)
    for k in range(n_row_chunks):
        so, po = row_owner(k)

        @pl.when(jnp.logical_or(so != s, po != p))
        def _():
            slot = rows.at[pl.ds(k * chunk, chunk)]
            pltpu.make_async_remote_copy(
                src_ref=slot, dst_ref=slot, send_sem=row_send.at[0], recv_sem=row_recv.at[k],
                device_id=core_peer, device_id_type=MESH).wait_recv()

    row_spec = rows[...]
    col_spec = cols[...]
    turned = jnp.concatenate([row_spec[:, n_all:], -row_spec[:, :n_all]], axis=1)
    highest = lax.Precision.HIGHEST
    out[0] = lax.dot_general(row_spec, col_spec, nt, precision=highest,
                             preferred_element_type=jnp.float32) * (1.0 / n_all)
    out[1] = lax.dot_general(turned, col_spec, nt, precision=highest,
                             preferred_element_type=jnp.float32) * (1.0 / n_all)
    if n_own < n_pan:
        pl.when(owner)(own_done)
    else:
        own_done()


def shards(sources, panel_geom, mic_pos, mic_order):
    n_seg = lax.axis_size("seg")
    n_pan = lax.axis_size("pan")
    segs_here = sources.shape[2]
    panels = sources.shape[3]
    n_mic = mic_pos.shape[1]
    n_split = n_seg // 2
    half = panels // n_split
    block = n_mic // n_seg
    chunk = max(8, block // n_pan)
    n_own = block // chunk
    rows_per = n_mic // n_pan
    n_red = n_split * n_pan
    width = 2 * n_seg * segs_here
    pieces = half // 256
    cfg = (n_seg, n_pan, segs_here, half, block, chunk, n_own, rows_per, pieces)
    f32, bf16 = jnp.float32, jnp.bfloat16
    dma = pltpu.SemaphoreType.DMA
    vmem = pl.BlockSpec(memory_space=pltpu.VMEM)
    mic_here = n_split * block
    return pl.pallas_call(
        functools.partial(kernel, cfg),
        out_shape=jax.ShapeDtypeStruct((2, rows_per, block), f32),
        in_specs=[pl.BlockSpec(memory_space=pltpu.HBM)] * 4,
        out_specs=vmem,
        scratch_shapes=[
            pltpu.VMEM((2, 2, n_seg * segs_here, half), bf16),
            pltpu.VMEM((6, half), f32),
            pltpu.VMEM((3, n_mic), f32),
            pltpu.VMEM((1, n_mic), jnp.int32),
            pltpu.VMEM((8, half), f32),
            pltpu.VMEM((3, mic_here, LANES), f32),
            pltpu.VMEM((4, mic_here, half // 2), bf16),
            pltpu.VMEM((4, mic_here, half // 2), bf16),
            pltpu.VMEM((mic_here, width), f32),
            pltpu.VMEM((mic_here, width), f32),
            pltpu.VMEM((n_split, block, width), f32),
            pltpu.VMEM((n_red, chunk, width), f32),
            pltpu.VMEM((chunk, width), f32),
            pltpu.VMEM((block, width), f32),
            pltpu.VMEM((rows_per, width), f32),
            dma((4,)), dma((2,)),
            dma((n_split - 1, pieces)), dma((n_split - 1, pieces)),
            dma((n_split - 1, pieces)), dma((n_split - 1, pieces)),
            dma((n_red,)), dma((n_red,)),
            dma((n_pan,)), dma((n_pan,)),
            dma((n_seg,)), dma((rows_per // chunk,)),
        ],
        compiler_params=pltpu.CompilerParams(
            collective_id=0, has_side_effects=True, vmem_limit_bytes=48 * 2**20),
        cost_estimate=pl.CostEstimate(
            flops=2 * 4 * mic_here * half * width, bytes_accessed=2**21,
            transcendentals=mic_here * half),
    )(sources, panel_geom, mic_pos, mic_order.reshape(1, n_mic))


def solution(mesh):
    placed = (P(None, None, "seg", "pan"), P(None, "pan"), P(), P())
    return jax.shard_map(
        shards, mesh=mesh, in_specs=placed, out_specs=P(None, "pan", "seg"), check_vma=False
    )
```

```python
import functools
import math

import jax
import jax.numpy as jnp
import numpy as np
from jax import lax
from jax.experimental import pallas as pl
from jax.experimental.pallas import tpu as pltpu
from jax.sharding import PartitionSpec as P

mach_number = 0.3
beta_sq = 0.91
wave_number = 40.0

MESH = pl.DeviceIdType.MESH
LANES = 128
SUB_ROWS = 32
TURN = wave_number / (beta_sq * 2.0 * math.pi)
BETA = math.sqrt(beta_sq)


def fit(function, degree_even, half_range, odd):
    count = degree_even + 1
    nodes = np.cos((np.arange(200) + 0.5) * math.pi / 200)
    u = (nodes + 1) / 2 * half_range**2
    x = np.sqrt(u)
    y = function(x) / x if odd else function(x)
    cheb = np.polynomial.chebyshev.Chebyshev.fit(
        u, y, count - 1, domain=[0, half_range**2]
    )
    return [float(v) for v in cheb.convert(kind=np.polynomial.Polynomial).coef]


ROOT2 = math.sqrt(2.0)
SIN_COEF = fit(lambda x: -ROOT2 * np.sin(math.pi * x), 3, 0.5, True)
COS_COEF = fit(lambda x: ROOT2 * np.cos(math.pi * x), 4, 0.5, False)


def horner(coef, u):
    total = coef[-1]
    for c in coef[-2::-1]:
        total = total * u + c
    return total


def pair_terms(mx, my, mz, panel):
    cx, cy, cz, n0, n1, n2 = panel
    dx = mx - cx
    dy = my - cy
    dz = mz - cz
    sq = dx * dx + (dy * dy + dz * dz)
    inv = lax.rsqrt(sq)
    turns = sq * inv - mach_number * dx
    magic = 12582912.0
    whole = (turns + magic) - magic
    f = turns - whole
    u = f * f
    s = horner(SIN_COEF, u) * f
    c = horner(COS_COEF, u)
    amplitude = inv * (TURN / (4.0 * math.pi))
    green_re = amplitude * (1.0 - s * s)
    green_im = amplitude * (s * c)
    normal_part = (dx * n0 + (dy * n1 + dz * n2)) * inv
    near = inv * (TURN / wave_number)
    dip_re = normal_part * (near * green_re - green_im)
    dip_im = normal_part * (near * green_im + green_re)
    return green_re, green_im, dip_re, dip_im


def kernel(cfg, src, geom_hbm, mics_hbm, order_hbm, out, src_buf, geom, mics, order, geo, micb,
           g_buf, r1, r2, spec, rs_buf, own, cols, rows, loc_sem, core_sems, y_send, y_recv, f_send, f_recv,
           rs_send, rs_recv, col_send, col_recv, row_send, row_recv):
    n_seg, n_pan, segs_here, half, block, chunk, n_own, rows_per, pieces = cfg
    n_split = n_seg // 2
    n_red = n_split * n_pan
    n_row_chunks = rows_per // chunk
    s = lax.axis_index("seg")
    p = lax.axis_index("pan")
    y = s // 2
    c = lax.rem(s, 2)
    me = y * n_pan + p
    core_peer = (y * 2 + 1 - c, p)
    m_own = s * block + chunk * p
    p_r = m_own // rows_per
    row_slot = (m_own - p_r * rows_per) // chunk
    owner = p < n_own

    def row_owner(k):
        m = rows_per * p + chunk * k
        so = m // block
        return so, (m - so * block) // chunk

    barrier = pltpu.get_barrier_semaphore()

    def tell(k, carry):
        t = lax.rem(me + k, n_red)
        pl.semaphore_signal(barrier, inc=1, device_id=((t // n_pan) * 2 + c, lax.rem(t, n_pan)),
                            device_id_type=MESH)
        return carry

    lax.fori_loop(1, n_red, tell, 0)
    pl.semaphore_signal(barrier, inc=1, device_id=core_peer, device_id_type=MESH)
    for k in range(n_row_chunks):
        so, po = row_owner(k)

        @pl.when(jnp.logical_or(so != s, po != p))
        def _():
            pl.semaphore_signal(barrier, inc=1, device_id=(so, po), device_id_type=MESH)

    here = pl.ds(pl.multiple_of(y * half, LANES), half)
    fetches = [
        pltpu.make_async_copy(order_hbm, order, loc_sem.at[1]),
        pltpu.make_async_copy(mics_hbm, mics, loc_sem.at[2]),
        pltpu.make_async_copy(geom_hbm.at[:, here], geom, loc_sem.at[3]),
    ]
    for fetch in fetches:
        fetch.start()
    for fetch in fetches:
        fetch.wait()

    positions = mics[...]
    part1 = positions.astype(jnp.bfloat16)
    rest = positions - part1.astype(jnp.float32)
    part2 = rest.astype(jnp.bfloat16)
    part3 = (rest - part2.astype(jnp.float32)).astype(jnp.bfloat16)
    n_mic = positions.shape[1]
    for b in range(n_split):
        listed = order[:, pl.ds(pl.multiple_of((2 * b + c) * block, LANES), block)]
        hot = (lax.broadcasted_iota(jnp.int32, (n_mic, block), 0) == listed)
        hot = jnp.where(hot, 1.0, 0.0).astype(jnp.bfloat16)
        chosen = sum(jnp.dot(q, hot, preferred_element_type=jnp.float32)
                     for q in (part1, part2, part3))
        for axis in range(3):
            scaled = chosen[axis:axis + 1] * (TURN if axis == 0 else TURN * BETA)
            for at in range(0, block, LANES):
                tile = jnp.broadcast_to(scaled[:, at:at + LANES], (LANES, LANES))
                micb[axis, pl.ds(b * block + at, LANES), :] = tile.T
    for r, scale in enumerate((TURN, TURN * BETA, TURN * BETA, 1.0, 1.0 / BETA, 1.0 / BETA)):
        geo[r:r + 1, :] = geom[r:r + 1, :] * scale

    own_rows_sent = jnp.where(p_r == p, n_seg - 1, n_seg)
    if n_own < n_pan:
        own_rows_sent = jnp.where(owner, own_rows_sent, 0)
    pl.semaphore_wait(barrier, n_red + own_rows_sent)

    def seg_rows(index):
        return pl.ds(pl.multiple_of(index * segs_here, 16), segs_here)

    piece = half // pieces

    def y_copy(k, j):
        yy = lax.rem(y + k, n_split)
        start = pl.multiple_of(yy * half + j * piece, LANES)
        return pltpu.make_async_remote_copy(
            src_ref=src.at[:, :, :, pl.ds(start, piece)],
            dst_ref=src_buf.at[:, :, seg_rows(s), pl.ds(pl.multiple_of(j * piece, LANES), piece)],
            send_sem=y_send.at[k - 1, j], recv_sem=y_recv.at[k - 1, j],
            device_id=(yy * 2 + c, p), device_id_type=MESH)

    def y_from(k):
        return lax.rem(y + n_split - k, n_split) * 2 + c

    def forward(k, j, cc):
        at = lax.rem(y + n_split - k, n_split) * 2 + cc
        ref = src_buf.at[:, :, seg_rows(at), pl.ds(pl.multiple_of(j * piece, LANES), piece)]
        return pltpu.make_async_remote_copy(
            src_ref=ref, dst_ref=ref, send_sem=f_send.at[k - 1, j], recv_sem=f_recv.at[k - 1, j],
            device_id=core_peer, device_id_type=MESH)

    def start_y(j, carry):
        for k in range(1, n_split):
            y_copy(k, j).start()
        return carry

    lax.fori_loop(0, pieces, start_y, 0)
    core_copy = pltpu.make_async_remote_copy(
        src_ref=src.at[:, :, :, here], dst_ref=src_buf.at[:, :, seg_rows(s), :],
        send_sem=core_sems.at[0], recv_sem=core_sems.at[1],
        device_id=core_peer, device_id_type=MESH)
    core_copy.start()
    local_copy = pltpu.make_async_copy(
        src.at[:, :, :, here], src_buf.at[:, :, seg_rows(s), :], loc_sem.at[0])
    local_copy.start()

    mic_here = n_split * block
    body_rows = min(256, mic_here)
    nt = (((1,), (1,)), ((), ()))

    parts = mic_here // body_rows

    def pairs(step, carry):
        lane = pl.multiple_of((step // parts) * LANES, LANES)
        base = lax.rem(step, parts) * body_rows
        panel = [jnp.broadcast_to(geo[r:r + 1, pl.ds(lane, LANES)], (SUB_ROWS, LANES))
                 for r in range(6)]
        for q in range(body_rows // SUB_ROWS):
            at = pl.ds(pl.multiple_of(base + q * SUB_ROWS, SUB_ROWS), SUB_ROWS)
            terms = pair_terms(micb[0, at, :], micb[1, at, :], micb[2, at, :], panel)
            for i in range(4):
                g_buf[i, at, pl.ds(lane, LANES)] = terms[i].astype(jnp.bfloat16)
        return carry

    steps = (piece // LANES) * parts
    for j in range(pieces):
        lax.fori_loop(j * steps, (j + 1) * steps, pairs, 0)
        for k in range(1, n_split):
            y_copy(k, j).wait_recv()
            forward(k, j, c).start()

    local_copy.wait()
    core_copy.wait()
    for j in range(pieces):
        for k in range(1, n_split):
            y_copy(k, j).wait_send()
            forward(k, j, c).wait_send()
            forward(k, j, 1 - c).wait_recv()
        at = pl.ds(j * piece, piece)
        mono = jnp.concatenate([src_buf[0, 0, :, at], src_buf[1, 0, :, at]], axis=0)
        dipole = jnp.concatenate([src_buf[0, 1, :, at], src_buf[1, 1, :, at]], axis=0)
        for first, total in ((0, r1), (1, r2)):
            term = lax.dot_general(g_buf[first, :, at], mono, nt,
                                   preferred_element_type=jnp.float32)
            term += lax.dot_general(g_buf[first + 2, :, at], dipole, nt,
                                    preferred_element_type=jnp.float32)
            total[...] = term if j == 0 else total[...] + term

    n_all = n_seg * segs_here
    for b in range(n_split):
        band = pl.ds(b * block, block)
        spec[b, :, :n_all] = r1[band, :n_all] - r2[band, n_all:]
        spec[b, :, n_all:] = r1[band, n_all:] + r2[band, :n_all]

    def rs_copy(t):
        ty = t // n_pan
        tp = lax.rem(t, n_pan)
        return tp, pltpu.make_async_remote_copy(
            src_ref=spec.at[ty, pl.ds(pl.multiple_of(tp * chunk, 8), chunk)],
            dst_ref=rs_buf.at[me], send_sem=rs_send.at[t], recv_sem=rs_recv.at[me],
            device_id=(ty * 2 + c, tp), device_id_type=MESH)

    def each_rs(action):
        def go(k, carry):
            tp, copy = rs_copy(lax.rem(me + k, n_red))
            if n_own < n_pan:
                pl.when(tp < n_own)(lambda: action(copy))
            else:
                action(copy)
            return carry

        lax.fori_loop(1, n_red, go, 0)

    each_rs(lambda copy: copy.start())

    def own_slot(ref):
        return ref.at[pl.ds(pl.multiple_of(p * chunk, 8), chunk)]

    def col_copy(q):
        return pltpu.make_async_remote_copy(
            src_ref=own, dst_ref=own_slot(cols), send_sem=col_send.at[q], recv_sem=col_recv.at[p],
            device_id=(s, q), device_id_type=MESH)

    def row_copy(q):
        return pltpu.make_async_remote_copy(
            src_ref=own, dst_ref=rows.at[pl.ds(pl.multiple_of(row_slot * chunk, 8), chunk)],
            send_sem=row_send.at[q], recv_sem=row_recv.at[row_slot],
            device_id=(q, p_r), device_id_type=MESH)

    def each_col(action):
        def go(k, carry):
            action(lax.rem(p + k, n_pan))
            return carry

        lax.fori_loop(1, n_pan, go, 0)

    def each_row(action):
        for k in range(n_seg):
            q = lax.rem(s + k, n_seg)
            if k == 0:
                pl.when(p_r != p)(lambda: action(row_copy(q)))
            else:
                action(row_copy(q))

    def own_sum():
        rs_buf[me] = spec[y, pl.ds(pl.multiple_of(p * chunk, 8), chunk), :]

        def arrived(k, carry):
            t = lax.rem(me + k, n_red)
            pltpu.make_async_remote_copy(
                src_ref=rs_buf.at[t], dst_ref=rs_buf.at[t], send_sem=rs_send.at[t],
                recv_sem=rs_recv.at[t], device_id=core_peer, device_id_type=MESH).wait_recv()
            return carry

        lax.fori_loop(1, n_red, arrived, 0)
        own[...] = jnp.sum(rs_buf[...], axis=0)
        each_col(lambda q: col_copy(q).start())
        each_row(lambda copy: copy.start())
        cols[pl.ds(pl.multiple_of(p * chunk, 8), chunk), :] = own[...]

        @pl.when(p_r == p)
        def _():
            rows[pl.ds(pl.multiple_of(row_slot * chunk, 8), chunk), :] = own[...]

    def own_done():
        each_col(lambda q: col_copy(q).wait_send())
        each_row(lambda copy: copy.wait_send())

    if n_own < n_pan:
        pl.when(owner)(own_sum)
    else:
        own_sum()

    each_rs(lambda copy: copy.wait_send())

    def col_arrived(k, carry):
        q = lax.rem(p + k, n_pan)

        def wait():
            slot = cols.at[pl.ds(pl.multiple_of(q * chunk, 8), chunk)]
            pltpu.make_async_remote_copy(
                src_ref=slot, dst_ref=slot, send_sem=col_send.at[q], recv_sem=col_recv.at[q],
                device_id=core_peer, device_id_type=MESH).wait_recv()

        if n_own < n_pan:
            pl.when(q < n_own)(wait)
        else:
            wait()
        return carry

    lax.fori_loop(1, n_pan, col_arrived, 0)
    for k in range(n_row_chunks):
        so, po = row_owner(k)

        @pl.when(jnp.logical_or(so != s, po != p))
        def _():
            slot = rows.at[pl.ds(k * chunk, chunk)]
            pltpu.make_async_remote_copy(
                src_ref=slot, dst_ref=slot, send_sem=row_send.at[0], recv_sem=row_recv.at[k],
                device_id=core_peer, device_id_type=MESH).wait_recv()

    row_spec = rows[...]
    col_spec = cols[...]
    turned = jnp.concatenate([row_spec[:, n_all:], -row_spec[:, :n_all]], axis=1)
    highest = lax.Precision.HIGHEST
    out[0] = lax.dot_general(row_spec, col_spec, nt, precision=highest,
                             preferred_element_type=jnp.float32) * (1.0 / n_all)
    out[1] = lax.dot_general(turned, col_spec, nt, precision=highest,
                             preferred_element_type=jnp.float32) * (1.0 / n_all)
    if n_own < n_pan:
        pl.when(owner)(own_done)
    else:
        own_done()


def shards(sources, panel_geom, mic_pos, mic_order):
    n_seg = lax.axis_size("seg")
    n_pan = lax.axis_size("pan")
    segs_here = sources.shape[2]
    panels = sources.shape[3]
    n_mic = mic_pos.shape[1]
    n_split = n_seg // 2
    half = panels // n_split
    block = n_mic // n_seg
    chunk = max(8, block // n_pan)
    n_own = block // chunk
    rows_per = n_mic // n_pan
    n_red = n_split * n_pan
    width = 2 * n_seg * segs_here
    pieces = 4
    cfg = (n_seg, n_pan, segs_here, half, block, chunk, n_own, rows_per, pieces)
    f32, bf16 = jnp.float32, jnp.bfloat16
    dma = pltpu.SemaphoreType.DMA
    vmem = pl.BlockSpec(memory_space=pltpu.VMEM)
    mic_here = n_split * block
    return pl.pallas_call(
        functools.partial(kernel, cfg),
        out_shape=jax.ShapeDtypeStruct((2, rows_per, block), f32),
        in_specs=[pl.BlockSpec(memory_space=pltpu.HBM)] * 4,
        out_specs=vmem,
        scratch_shapes=[
            pltpu.VMEM((2, 2, n_seg * segs_here, half), bf16),
            pltpu.VMEM((6, half), f32),
            pltpu.VMEM((3, n_mic), f32),
            pltpu.VMEM((1, n_mic), jnp.int32),
            pltpu.VMEM((8, half), f32),
            pltpu.VMEM((3, mic_here, LANES), f32),
            pltpu.VMEM((4, mic_here, half), bf16),
            pltpu.VMEM((mic_here, width), f32),
            pltpu.VMEM((mic_here, width), f32),
            pltpu.VMEM((n_split, block, width), f32),
            pltpu.VMEM((n_red, chunk, width), f32),
            pltpu.VMEM((chunk, width), f32),
            pltpu.VMEM((block, width), f32),
            pltpu.VMEM((rows_per, width), f32),
            dma((4,)), dma((2,)),
            dma((n_split - 1, pieces)), dma((n_split - 1, pieces)),
            dma((n_split - 1, pieces)), dma((n_split - 1, pieces)),
            dma((n_red,)), dma((n_red,)),
            dma((n_pan,)), dma((n_pan,)),
            dma((n_seg,)), dma((rows_per // chunk,)),
        ],
        compiler_params=pltpu.CompilerParams(
            collective_id=0, has_side_effects=True, vmem_limit_bytes=48 * 2**20),
        cost_estimate=pl.CostEstimate(
            flops=2 * 4 * mic_here * half * width, bytes_accessed=2**21,
            transcendentals=mic_here * half),
    )(sources, panel_geom, mic_pos, mic_order.reshape(1, n_mic))


def solution(mesh):
    placed = (P(None, None, "seg", "pan"), P(None, "pan"), P(), P())
    return jax.shard_map(
        shards, mesh=mesh, in_specs=placed, out_specs=P(None, "pan", "seg"), check_vma=False
    )
```

```python
import functools
import math

import jax
import jax.numpy as jnp
import numpy as np
from jax import lax
from jax.experimental import pallas as pl
from jax.experimental.pallas import tpu as pltpu
from jax.sharding import PartitionSpec as P

mach_number = 0.3
beta_sq = 0.91
wave_number = 40.0

MESH = pl.DeviceIdType.MESH
LANES = 128
SUB_ROWS = 32
TURN = wave_number / (beta_sq * 2.0 * math.pi)
BETA = math.sqrt(beta_sq)


def fit(function, degree_even, half_range, odd):
    count = degree_even + 1
    nodes = np.cos((np.arange(200) + 0.5) * math.pi / 200)
    u = (nodes + 1) / 2 * half_range**2
    x = np.sqrt(u)
    y = function(x) / x if odd else function(x)
    cheb = np.polynomial.chebyshev.Chebyshev.fit(
        u, y, count - 1, domain=[0, half_range**2]
    )
    return [float(v) for v in cheb.convert(kind=np.polynomial.Polynomial).coef]


ROOT2 = math.sqrt(2.0)
SIN_COEF = fit(lambda x: -ROOT2 * np.sin(math.pi * x), 3, 0.5, True)
COS_COEF = fit(lambda x: ROOT2 * np.cos(math.pi * x), 4, 0.5, False)


def horner(coef, u):
    total = coef[-1]
    for c in coef[-2::-1]:
        total = total * u + c
    return total


def pair_terms(mx, my, mz, panel):
    cx, cy, cz, n0, n1, n2 = panel
    dx = mx - cx
    dy = my - cy
    dz = mz - cz
    sq = dx * dx + (dy * dy + dz * dz)
    inv = lax.rsqrt(sq)
    turns = sq * inv - mach_number * dx
    magic = 12582912.0
    whole = (turns + magic) - magic
    f = turns - whole
    u = f * f
    s = horner(SIN_COEF, u) * f
    c = horner(COS_COEF, u)
    amplitude = inv * (TURN / (4.0 * math.pi))
    green_re = amplitude * (1.0 - s * s)
    green_im = amplitude * (s * c)
    normal_part = (dx * n0 + (dy * n1 + dz * n2)) * inv
    near = inv * (TURN / wave_number)
    dip_re = normal_part * (near * green_re - green_im)
    dip_im = normal_part * (near * green_im + green_re)
    return green_re, green_im, dip_re, dip_im


def kernel(cfg, src, geom_hbm, mics_hbm, order_hbm, out, src_buf, geom, mics, order, geo, micb,
           g_buf, r1, r2, spec, rs_buf, own, cols, rows, loc_sem, core_sems, y_send, y_recv, f_send, f_recv,
           rs_send, rs_recv, col_send, col_recv, row_send, row_recv):
    n_seg, n_pan, segs_here, half, block, chunk, n_own, rows_per, pieces = cfg
    n_split = n_seg // 2
    n_red = n_split * n_pan
    n_row_chunks = rows_per // chunk
    s = lax.axis_index("seg")
    p = lax.axis_index("pan")
    y = s // 2
    c = lax.rem(s, 2)
    me = y * n_pan + p
    core_peer = (y * 2 + 1 - c, p)
    m_own = s * block + chunk * p
    p_r = m_own // rows_per
    row_slot = (m_own - p_r * rows_per) // chunk
    owner = p < n_own

    def row_owner(k):
        m = rows_per * p + chunk * k
        so = m // block
        return so, (m - so * block) // chunk

    barrier = pltpu.get_barrier_semaphore()

    def tell(k, carry):
        t = lax.rem(me + k, n_red)
        pl.semaphore_signal(barrier, inc=1, device_id=((t // n_pan) * 2 + c, lax.rem(t, n_pan)),
                            device_id_type=MESH)
        return carry

    lax.fori_loop(1, n_red, tell, 0)
    pl.semaphore_signal(barrier, inc=1, device_id=core_peer, device_id_type=MESH)
    for k in range(n_row_chunks):
        so, po = row_owner(k)

        @pl.when(jnp.logical_or(so != s, po != p))
        def _():
            pl.semaphore_signal(barrier, inc=1, device_id=(so, po), device_id_type=MESH)

    here = pl.ds(pl.multiple_of(y * half, LANES), half)
    fetches = [
        pltpu.make_async_copy(order_hbm, order, loc_sem.at[1]),
        pltpu.make_async_copy(mics_hbm, mics, loc_sem.at[2]),
        pltpu.make_async_copy(geom_hbm.at[:, here], geom, loc_sem.at[3]),
    ]
    for fetch in fetches:
        fetch.start()
    for fetch in fetches:
        fetch.wait()

    positions = mics[...]
    part1 = positions.astype(jnp.bfloat16)
    rest = positions - part1.astype(jnp.float32)
    part2 = rest.astype(jnp.bfloat16)
    part3 = (rest - part2.astype(jnp.float32)).astype(jnp.bfloat16)
    n_mic = positions.shape[1]
    for b in range(n_split):
        listed = order[:, pl.ds(pl.multiple_of((2 * b + c) * block, LANES), block)]
        hot = (lax.broadcasted_iota(jnp.int32, (n_mic, block), 0) == listed)
        hot = jnp.where(hot, 1.0, 0.0).astype(jnp.bfloat16)
        chosen = sum(jnp.dot(q, hot, preferred_element_type=jnp.float32)
                     for q in (part1, part2, part3))
        for axis in range(3):
            scaled = chosen[axis:axis + 1] * (TURN if axis == 0 else TURN * BETA)
            for at in range(0, block, LANES):
                tile = jnp.broadcast_to(scaled[:, at:at + LANES], (LANES, LANES))
                micb[axis, pl.ds(b * block + at, LANES), :] = tile.T
    for r, scale in enumerate((TURN, TURN * BETA, TURN * BETA, 1.0, 1.0 / BETA, 1.0 / BETA)):
        geo[r:r + 1, :] = geom[r:r + 1, :] * scale

    own_rows_sent = jnp.where(p_r == p, n_seg - 1, n_seg)
    if n_own < n_pan:
        own_rows_sent = jnp.where(owner, own_rows_sent, 0)
    pl.semaphore_wait(barrier, n_red + own_rows_sent)

    def seg_rows(index):
        return pl.ds(pl.multiple_of(index * segs_here, 16), segs_here)

    piece = half // pieces

    def y_copy(k, j):
        yy = lax.rem(y + k, n_split)
        start = pl.multiple_of(yy * half + j * piece, LANES)
        return pltpu.make_async_remote_copy(
            src_ref=src.at[:, :, :, pl.ds(start, piece)],
            dst_ref=src_buf.at[:, :, seg_rows(s), pl.ds(pl.multiple_of(j * piece, LANES), piece)],
            send_sem=y_send.at[k - 1, j], recv_sem=y_recv.at[k - 1, j],
            device_id=(yy * 2 + c, p), device_id_type=MESH)

    def y_from(k):
        return lax.rem(y + n_split - k, n_split) * 2 + c

    def forward(k, j, cc):
        at = lax.rem(y + n_split - k, n_split) * 2 + cc
        ref = src_buf.at[:, :, seg_rows(at), pl.ds(pl.multiple_of(j * piece, LANES), piece)]
        return pltpu.make_async_remote_copy(
            src_ref=ref, dst_ref=ref, send_sem=f_send.at[k - 1, j], recv_sem=f_recv.at[k - 1, j],
            device_id=core_peer, device_id_type=MESH)

    def start_y(j, carry):
        for k in range(1, n_split):
            y_copy(k, j).start()
        return carry

    lax.fori_loop(0, pieces, start_y, 0)
    core_copy = pltpu.make_async_remote_copy(
        src_ref=src.at[:, :, :, here], dst_ref=src_buf.at[:, :, seg_rows(s), :],
        send_sem=core_sems.at[0], recv_sem=core_sems.at[1],
        device_id=core_peer, device_id_type=MESH)
    core_copy.start()
    local_copy = pltpu.make_async_copy(
        src.at[:, :, :, here], src_buf.at[:, :, seg_rows(s), :], loc_sem.at[0])
    local_copy.start()

    mic_here = n_split * block
    body_rows = min(512, mic_here)
    nt = (((1,), (1,)), ((), ()))

    parts = mic_here // body_rows

    def pairs(step, carry):
        lane = pl.multiple_of((step // parts) * LANES, LANES)
        base = lax.rem(step, parts) * body_rows
        panel = [jnp.broadcast_to(geo[r:r + 1, pl.ds(lane, LANES)], (SUB_ROWS, LANES))
                 for r in range(6)]
        for q in range(body_rows // SUB_ROWS):
            at = pl.ds(pl.multiple_of(base + q * SUB_ROWS, SUB_ROWS), SUB_ROWS)
            terms = pair_terms(micb[0, at, :], micb[1, at, :], micb[2, at, :], panel)
            for i in range(4):
                g_buf[i, at, pl.ds(lane, LANES)] = terms[i].astype(jnp.bfloat16)
        return carry

    steps = (piece // LANES) * parts
    for j in range(pieces):
        lax.fori_loop(j * steps, (j + 1) * steps, pairs, 0)
        for k in range(1, n_split):
            y_copy(k, j).wait_recv()
            forward(k, j, c).start()

    local_copy.wait()
    core_copy.wait()
    for j in range(pieces):
        for k in range(1, n_split):
            y_copy(k, j).wait_send()
            forward(k, j, c).wait_send()
            forward(k, j, 1 - c).wait_recv()
        at = pl.ds(j * piece, piece)
        mono = jnp.concatenate([src_buf[0, 0, :, at], src_buf[1, 0, :, at]], axis=0)
        dipole = jnp.concatenate([src_buf[0, 1, :, at], src_buf[1, 1, :, at]], axis=0)
        for first, total in ((0, r1), (1, r2)):
            term = lax.dot_general(g_buf[first, :, at], mono, nt,
                                   preferred_element_type=jnp.float32)
            term += lax.dot_general(g_buf[first + 2, :, at], dipole, nt,
                                    preferred_element_type=jnp.float32)
            total[...] = term if j == 0 else total[...] + term

    n_all = n_seg * segs_here
    for b in range(n_split):
        band = pl.ds(b * block, block)
        spec[b, :, :n_all] = r1[band, :n_all] - r2[band, n_all:]
        spec[b, :, n_all:] = r1[band, n_all:] + r2[band, :n_all]

    def rs_copy(t):
        ty = t // n_pan
        tp = lax.rem(t, n_pan)
        return tp, pltpu.make_async_remote_copy(
            src_ref=spec.at[ty, pl.ds(pl.multiple_of(tp * chunk, 8), chunk)],
            dst_ref=rs_buf.at[me], send_sem=rs_send.at[t], recv_sem=rs_recv.at[me],
            device_id=(ty * 2 + c, tp), device_id_type=MESH)

    def each_rs(action):
        def go(k, carry):
            tp, copy = rs_copy(lax.rem(me + k, n_red))
            if n_own < n_pan:
                pl.when(tp < n_own)(lambda: action(copy))
            else:
                action(copy)
            return carry

        lax.fori_loop(1, n_red, go, 0)

    each_rs(lambda copy: copy.start())

    def own_slot(ref):
        return ref.at[pl.ds(pl.multiple_of(p * chunk, 8), chunk)]

    def col_copy(q):
        return pltpu.make_async_remote_copy(
            src_ref=own, dst_ref=own_slot(cols), send_sem=col_send.at[q], recv_sem=col_recv.at[p],
            device_id=(s, q), device_id_type=MESH)

    def row_copy(q):
        return pltpu.make_async_remote_copy(
            src_ref=own, dst_ref=rows.at[pl.ds(pl.multiple_of(row_slot * chunk, 8), chunk)],
            send_sem=row_send.at[q], recv_sem=row_recv.at[row_slot],
            device_id=(q, p_r), device_id_type=MESH)

    def each_col(action):
        def go(k, carry):
            action(lax.rem(p + k, n_pan))
            return carry

        lax.fori_loop(1, n_pan, go, 0)

    def each_row(action):
        for k in range(n_seg):
            q = lax.rem(s + k, n_seg)
            if k == 0:
                pl.when(p_r != p)(lambda: action(row_copy(q)))
            else:
                action(row_copy(q))

    def own_sum():
        rs_buf[me] = spec[y, pl.ds(pl.multiple_of(p * chunk, 8), chunk), :]

        def arrived(k, carry):
            t = lax.rem(me + k, n_red)
            pltpu.make_async_remote_copy(
                src_ref=rs_buf.at[t], dst_ref=rs_buf.at[t], send_sem=rs_send.at[t],
                recv_sem=rs_recv.at[t], device_id=core_peer, device_id_type=MESH).wait_recv()
            return carry

        lax.fori_loop(1, n_red, arrived, 0)
        own[...] = jnp.sum(rs_buf[...], axis=0)
        each_col(lambda q: col_copy(q).start())
        each_row(lambda copy: copy.start())
        cols[pl.ds(pl.multiple_of(p * chunk, 8), chunk), :] = own[...]

        @pl.when(p_r == p)
        def _():
            rows[pl.ds(pl.multiple_of(row_slot * chunk, 8), chunk), :] = own[...]

    def own_done():
        each_col(lambda q: col_copy(q).wait_send())
        each_row(lambda copy: copy.wait_send())

    if n_own < n_pan:
        pl.when(owner)(own_sum)
    else:
        own_sum()

    each_rs(lambda copy: copy.wait_send())

    def col_arrived(k, carry):
        q = lax.rem(p + k, n_pan)

        def wait():
            slot = cols.at[pl.ds(pl.multiple_of(q * chunk, 8), chunk)]
            pltpu.make_async_remote_copy(
                src_ref=slot, dst_ref=slot, send_sem=col_send.at[q], recv_sem=col_recv.at[q],
                device_id=core_peer, device_id_type=MESH).wait_recv()

        if n_own < n_pan:
            pl.when(q < n_own)(wait)
        else:
            wait()
        return carry

    lax.fori_loop(1, n_pan, col_arrived, 0)
    for k in range(n_row_chunks):
        so, po = row_owner(k)

        @pl.when(jnp.logical_or(so != s, po != p))
        def _():
            slot = rows.at[pl.ds(k * chunk, chunk)]
            pltpu.make_async_remote_copy(
                src_ref=slot, dst_ref=slot, send_sem=row_send.at[0], recv_sem=row_recv.at[k],
                device_id=core_peer, device_id_type=MESH).wait_recv()

    row_spec = rows[...]
    col_spec = cols[...]
    turned = jnp.concatenate([row_spec[:, n_all:], -row_spec[:, :n_all]], axis=1)
    highest = lax.Precision.HIGHEST
    out[0] = lax.dot_general(row_spec, col_spec, nt, precision=highest,
                             preferred_element_type=jnp.float32) * (1.0 / n_all)
    out[1] = lax.dot_general(turned, col_spec, nt, precision=highest,
                             preferred_element_type=jnp.float32) * (1.0 / n_all)
    if n_own < n_pan:
        pl.when(owner)(own_done)
    else:
        own_done()


def shards(sources, panel_geom, mic_pos, mic_order):
    n_seg = lax.axis_size("seg")
    n_pan = lax.axis_size("pan")
    segs_here = sources.shape[2]
    panels = sources.shape[3]
    n_mic = mic_pos.shape[1]
    n_split = n_seg // 2
    half = panels // n_split
    block = n_mic // n_seg
    chunk = max(8, block // n_pan)
    n_own = block // chunk
    rows_per = n_mic // n_pan
    n_red = n_split * n_pan
    width = 2 * n_seg * segs_here
    pieces = 4
    cfg = (n_seg, n_pan, segs_here, half, block, chunk, n_own, rows_per, pieces)
    f32, bf16 = jnp.float32, jnp.bfloat16
    dma = pltpu.SemaphoreType.DMA
    vmem = pl.BlockSpec(memory_space=pltpu.VMEM)
    mic_here = n_split * block
    return pl.pallas_call(
        functools.partial(kernel, cfg),
        out_shape=jax.ShapeDtypeStruct((2, rows_per, block), f32),
        in_specs=[pl.BlockSpec(memory_space=pltpu.HBM)] * 4,
        out_specs=vmem,
        scratch_shapes=[
            pltpu.VMEM((2, 2, n_seg * segs_here, half), bf16),
            pltpu.VMEM((6, half), f32),
            pltpu.VMEM((3, n_mic), f32),
            pltpu.VMEM((1, n_mic), jnp.int32),
            pltpu.VMEM((8, half), f32),
            pltpu.VMEM((3, mic_here, LANES), f32),
            pltpu.VMEM((4, mic_here, half), bf16),
            pltpu.VMEM((mic_here, width), f32),
            pltpu.VMEM((mic_here, width), f32),
            pltpu.VMEM((n_split, block, width), f32),
            pltpu.VMEM((n_red, chunk, width), f32),
            pltpu.VMEM((chunk, width), f32),
            pltpu.VMEM((block, width), f32),
            pltpu.VMEM((rows_per, width), f32),
            dma((4,)), dma((2,)),
            dma((n_split - 1, pieces)), dma((n_split - 1, pieces)),
            dma((n_split - 1, pieces)), dma((n_split - 1, pieces)),
            dma((n_red,)), dma((n_red,)),
            dma((n_pan,)), dma((n_pan,)),
            dma((n_seg,)), dma((rows_per // chunk,)),
        ],
        compiler_params=pltpu.CompilerParams(
            collective_id=0, has_side_effects=True, vmem_limit_bytes=48 * 2**20),
        cost_estimate=pl.CostEstimate(
            flops=2 * 4 * mic_here * half * width, bytes_accessed=2**21,
            transcendentals=mic_here * half),
    )(sources, panel_geom, mic_pos, mic_order.reshape(1, n_mic))


def solution(mesh):
    placed = (P(None, None, "seg", "pan"), P(None, "pan"), P(), P())
    return jax.shard_map(
        shards, mesh=mesh, in_specs=placed, out_specs=P(None, "pan", "seg"), check_vma=False
    )
```
